512 devices in a mesh: in: 8 (over y, core), out: 8 (over z_hi, x), tok: 8 (over z_lo).
Axes of the slice: x: 4, y: 4, z: 16 (z_hi: 2, z_lo: 8; z = z_hi * 8 + z_lo), core: 2. Of those that a mesh axis runs over, the one named last changes fastest.
Arguments:
- tokens_in: bfloat16 [1024, 8192], P('tok', 'in'), may hold values from -6 to 6
- weight: bfloat16 [8192, 32768], P('in', ('out', 'tok')), may hold values from -0.0625 to 0.0625
- grad_out: bfloat16 [1024, 32768], P('tok', 'out'), may hold values from -6 to 6
Outputs:
- grad_input: bfloat16 [1024, 8192], P('tok', ('in', 'out'))
- grad_weight: bfloat16 [8192, 32768], P('in', ('out', 'tok'))
- act_factor: float32 [8192, 4096], P(('in', 'tok'), 'out')
- grad_factor: float32 [32768, 4096], P(('out', 'tok'), 'in')
The draws below stay inside these ranges and needn't reach their ends.
All inputs are finite; a program needn't handle non-finite values.
Results may differ from the reference program's by a relative error of at most 0.0049.
Values may be sent and summed in bfloat16 or wider, within the bound.
No kernel may reach another device: no remote copies, remote signals or barrier semaphores. Data moves between devices by JAX's collectives and lax.ppermute only.
A program may use at most 64 MiB of HBM per device.

```python
import math
import jax
import jax.numpy as jnp
from jax import lax

D = 8192
F = 32768
BLK = 4096
TOKENS = 1024


def levels(own_key, extent, cuts, least, largest):
    def one(axis_at, parts):
        steps = jax.random.uniform(jax.random.fold_in(jax.random.fold_in(own_key, 6), axis_at), (parts,), jnp.float32, least / len(cuts), largest / len(cuts))
        return jnp.repeat(jnp.exp(steps), extent[axis_at] // parts).reshape((-1,) + (1,) * (len(extent) - axis_at - 1))

    gain = one(*cuts[0])
    for cut in cuts[1:]:
        gain = gain * one(*cut)
    return gain


def bell_draw(key, extent, width, limit, shards=(), kind=jnp.bfloat16):
    entries = width * jax.random.normal(key, extent, jnp.float32)
    if shards:
        entries = entries * levels(key, extent, shards, -0.22, 0.18)
    return jnp.clip(entries, -limit, limit).astype(kind)


def setup_inputs(seed: int = 0) -> dict:
    key_list = jax.random.split(jax.random.key(seed), 4)
    return {
        "tokens_in": bell_draw(key_list[0], (TOKENS, D), 1.0, 6.0, ((0, 8), (1, 8))),
        "weight": bell_draw(key_list[1], (D, F), D ** -0.5, 0.0625, ((0, 8), (1, 64))),
        "grad_out": bell_draw(key_list[2], (TOKENS, F), 1.0, 6.0, ((0, 8), (1, 8))),
    }


def gelu_slope(values):
    scale = math.sqrt(2.0 / math.pi)
    cubic = values * values * values
    tanh_val = jnp.tanh(scale * (values + 0.044715 * cubic))
    return 0.5 * (1.0 + tanh_val) + 0.5 * values * (1.0 - tanh_val * tanh_val) * scale * (1.0 + 3.0 * 0.044715 * values * values)

def block_grams(matrix, blocks):
    stacked = matrix.astype(jnp.float32).reshape(TOKENS, blocks, BLK).transpose(1, 0, 2)

    def gram(piece):
        return jnp.dot(piece.T, piece, precision=lax.Precision.HIGHEST) / float(TOKENS)
    return lax.map(gram, stacked).reshape(blocks * BLK, BLK)

def reference(tokens_in, weight, grad_out):
    preact = jnp.dot(tokens_in, weight, preferred_element_type=jnp.float32)
    grad_pre = (grad_out.astype(jnp.float32) * gelu_slope(preact)).astype(jnp.bfloat16)
    grad_input = jnp.dot(grad_pre, weight.T, preferred_element_type=jnp.float32).astype(jnp.bfloat16)
    grad_weight = jnp.dot(tokens_in.T, grad_pre, preferred_element_type=jnp.float32).astype(jnp.bfloat16)
    act_factor = block_grams(tokens_in, D // BLK)
    grad_factor = block_grams(grad_pre, F // BLK)
    return (grad_input, grad_weight, act_factor, grad_factor)
```

```python
import math

import jax
import jax.numpy as jnp
from jax import lax
from jax.sharding import Mesh, PartitionSpec as P

BF16 = jnp.bfloat16
F16 = jnp.float16
F32 = jnp.float32
IN = ("y", "core")
OUT = ("zh", "x")
TOK = ("th", "tl")


def gelu_slope(values):
    scale = math.sqrt(2.0 / math.pi)
    cubic = values * values * values
    tanh_val = jnp.tanh(scale * (values + 0.044715 * cubic))
    return 0.5 * (1.0 + tanh_val) + 0.5 * values * (1.0 - tanh_val * tanh_val) * scale * (
        1.0 + 3.0 * 0.044715 * values * values
    )


def swap(value, axis):
    return lax.ppermute(value, axis, [(0, 1), (1, 0)])


def exchange(value, axis):
    return lax.all_to_all(value, axis, split_axis=0, concat_axis=0, tiled=True)


def spread(value, axis):
    size = lax.axis_size(axis)
    return exchange(jnp.broadcast_to(value[None], (size,) + value.shape), axis)


def total(parts):
    return jnp.sum(parts.astype(F32), axis=0)


def rows_of(value, start, size):
    return lax.dynamic_slice_in_dim(value, start, size, 0)


def cols_of(value, start, size):
    return lax.dynamic_slice_in_dim(value, start, size, 1)


def tn_dot(left, right):
    return lax.dot_general(left, right, (((0,), (0,)), ((), ())), preferred_element_type=F32)


def on_device(tokens_in, weight, grad_out):
    y, core, zh, x, th, tl = (lax.axis_index(a) for a in ("y", "core", "zh", "x", "th", "tl"))
    tok = th * 4 + tl
    piece = core * 4 + y

    with jax.named_scope("gather_tokens"):
        own = rows_of(tokens_in, x * 32, 32)
        other = swap(own, "th")
        both = jnp.where(th == 0, jnp.stack([own, other]), jnp.stack([other, own]))
        near = spread(both, "tl").reshape(4, 2, 2, 16, 1024).transpose(2, 1, 0, 3, 4)
        tokens = spread(near.reshape(256, 1024), "x").reshape(1024, 1024)

    with jax.named_scope("grad_out_piece"):
        own_rows = rows_of(grad_out, piece * 16, 16).reshape(16, 8, 512).transpose(1, 0, 2)
        grad_out_piece = exchange(own_rows, TOK).reshape(128, 512)

    with jax.named_scope("preact"):
        partial = jnp.dot(tokens, weight, preferred_element_type=F32).astype(F16)
        half = total(exchange(partial.reshape(2, 512, 512), "core")).astype(F16)
        preact = total(exchange(half.reshape(4, 128, 512), "y"))
        grad_piece = (grad_out_piece.astype(F32) * gelu_slope(preact)).astype(BF16)

    with jax.named_scope("gather_grad"):
        grad_half = spread(grad_piece, "y")
        grad_rows = spread(grad_half.reshape(512, 512), "core").reshape(1024, 512)

    with jax.named_scope("grad_input"):
        by_x = weight.reshape(2, 4, 128, 512).transpose(1, 0, 2, 3).reshape(4, 256, 512)
        share = jnp.einsum("rc,kfc->krf", grad_rows, by_x, preferred_element_type=F32).astype(BF16)
        part = total(exchange(share, "x")).astype(BF16)
        part = part.reshape(8, 2, 4, 16, 256).transpose(2, 0, 1, 3, 4)
        part = total(exchange(part, "tl")).astype(BF16)
        part = part.reshape(8, 2, 16, 2, 128).transpose(3, 1, 0, 2, 4).reshape(4, 128, 128)
        grad_input = total(exchange(part, ("zh", "th"))).astype(BF16)

    with jax.named_scope("grad_weight"):
        grad_weight = tn_dot(tokens, grad_rows).astype(BF16)

    with jax.named_scope("grad_factor"):
        pieces = lax.all_gather(grad_piece, TOK, axis=0, tiled=True)
        pieces = pieces.reshape(4, 2, 128, 512).transpose(1, 0, 2, 3).reshape(8, 128, 512)
        cross = exchange(pieces, ("core", "y")).reshape(1024, 512)
        grad_factor = tn_dot(grad_rows, cross) / 1024.0

    with jax.named_scope("act_factor"):
        act_cols = cols_of(tokens, x % 2 * 512, 512)
        act_cols = jnp.where(core == x // 2, act_cols, swap(act_cols, "core"))
        from_y = lax.ppermute(act_cols, "y", [(0, 1), (1, 0), (2, 3), (3, 2)])
        act_cols = jnp.where(y % 2 == zh, act_cols, from_y)
        act_factor = tn_dot(cols_of(tokens, tok * 128, 128), act_cols) / 1024.0
    return (grad_input, grad_weight, act_factor, grad_factor)


def solution(mesh):
    fine = Mesh(mesh.devices.reshape(4, 2, 2, 4, 2, 4), ("y", "core", "zh", "x", "th", "tl"))
    return jax.shard_map(
        on_device,
        mesh=fine,
        in_specs=(P(TOK, IN), P(IN, OUT + TOK), P(TOK, OUT)),
        out_specs=(P(TOK, IN + OUT), P(IN, OUT + TOK), P(IN + TOK, OUT), P(OUT + TOK, IN)),
        check_vma=False,
    )
```

```python
import math

import jax
import jax.numpy as jnp
from jax import lax
from jax.sharding import Mesh, PartitionSpec as P

BF16 = jnp.bfloat16
F16 = jnp.float16
F32 = jnp.float32
IN = ("y", "core")
OUT = ("zh", "x")
TOK = ("th", "tl")
SCALE = 4096.0


def gelu_slope(values):
    scale = math.sqrt(2.0 / math.pi)
    cubic = values * values * values
    tanh_val = jnp.tanh(scale * (values + 0.044715 * cubic))
    return 0.5 * (1.0 + tanh_val) + 0.5 * values * (1.0 - tanh_val * tanh_val) * scale * (
        1.0 + 3.0 * 0.044715 * values * values
    )


def swap(value, axis):
    return lax.ppermute(value, axis, [(0, 1), (1, 0)])


def ring(step):
    return [(i, (i + step) % 4) for i in range(4)]


def shift(value, step):
    return lax.ppermute(value, "x", ring(step))


def pick(values, at):
    low = jnp.where(at == 0, values[0], values[1])
    high = jnp.where(at == 2, values[2], values[3])
    return jnp.where(at < 2, low, high)


def skew(value, sign):
    pairs = [(k * 4 + i, k * 4 + (i + sign * k) % 4) for k in range(4) for i in range(4)]
    return lax.ppermute(value, ("y", "x"), pairs)


def exchange(value, axis):
    return lax.all_to_all(value, axis, split_axis=0, concat_axis=0, tiled=True)


def spread(value, axis):
    size = lax.axis_size(axis)
    return exchange(jnp.broadcast_to(value[None], (size,) + value.shape), axis)


def total(parts):
    return jnp.sum(parts.astype(F32), axis=0)


def rows_of(value, start, size):
    return lax.dynamic_slice_in_dim(value, start, size, 0)


def cols_of(value, start, size):
    return lax.dynamic_slice_in_dim(value, start, size, 1)


def both_th(own, other, th):
    return jnp.where(th == 0, jnp.stack([own, other]), jnp.stack([other, own]))


def dot(left, right):
    return jnp.dot(left, right, preferred_element_type=F32)


def nt_dot(left, right):
    return lax.dot_general(left, right, (((1,), (1,)), ((), ())), preferred_element_type=F32)


def tn_dot(left, right):
    return lax.dot_general(left, right, (((0,), (0,)), ((), ())), preferred_element_type=F32)


def on_device(tokens_in, weight, grad_out):
    y, core, x, th, tl = (lax.axis_index(a) for a in ("y", "core", "x", "th", "tl"))
    zh = lax.axis_index("zh")
    tok = th * 4 + tl

    with jax.named_scope("gather_weight"):
        after, before = shift(weight, -1), shift(weight, 1)
        far_top, far_low = shift(after[:512], -1), shift(before[512:], 1)
        far = jnp.concatenate([far_top, far_low], axis=0)
        weights = (weight, after, far, before)

    with jax.named_scope("gather_tokens"):
        own = rows_of(tokens_in, x * 32, 32)
        skewed = skew(rows_of(grad_out, (x - y) % 4 * 32 + core * 16, 16), -1)
        keep, send = cols_of(skewed, th * 2048, 2048), cols_of(skewed, (1 - th) * 2048, 2048)
        send = jnp.concatenate([own, send[:, :1024], send[:, 1024:]], axis=0)
        got = swap(send, "th")
        got_grad = jnp.concatenate([got[32:48], got[48:]], axis=1)
        near_grad = both_th(keep.reshape(16, 4, 512), got_grad.reshape(16, 4, 512), th)
        near_grad = near_grad.transpose(2, 1, 0, 3).reshape(4, 16, 1024)
        near = both_th(own, got[:32], th).reshape(64, 1024)
        near = jnp.concatenate([jnp.broadcast_to(near[None], (4, 64, 1024)), near_grad], axis=1)
        near = exchange(near, "tl")
        tokens = near[:, :64].reshape(4, 2, 2, 16, 1024).transpose(2, 1, 0, 3, 4).reshape(256, 1024)
        grad_out_piece = near[:, 64:].reshape(4, 16, 2, 512).transpose(2, 0, 1, 3).reshape(128, 512)

    with jax.named_scope("preact"):
        partial = [
            dot(tokens, weight),
            dot(tokens, after),
            dot(tokens[:, :512], far_top) + dot(tokens[:, 512:], far_low),
            dot(tokens, before),
        ]
        partial = jnp.stack([part.astype(F16) for part in partial])
        partial, late_tokens = lax.optimization_barrier((partial, tokens))
        preact = total(exchange(partial.reshape(8, 128, 512), IN))
        grad_piece = (grad_out_piece.astype(F32) * gelu_slope(preact)).astype(BF16)
        factor_piece = skew(grad_piece, 1)
        grad_piece, factor_piece = lax.optimization_barrier((grad_piece, factor_piece))

    with jax.named_scope("all_tokens"):
        all_tokens = [late_tokens] + [shift(late_tokens, k) for k in range(1, 4)]
        all_tokens = jnp.concatenate(all_tokens, axis=0)

    with jax.named_scope("gather_grad"):
        scaled = (grad_piece.astype(F32) * SCALE).astype(F16)
        grads = lax.all_gather(scaled, IN, axis=0, tiled=True).reshape(4, 256, 512)
        grads = (grads.astype(F32) * (1.0 / SCALE)).astype(BF16)

    with jax.named_scope("grad_input"):
        share = sum(nt_dot(grads[k], weights[k]) for k in range(4)).astype(BF16)
        share = share.reshape(2, 2, 4, 16, 1024).transpose(2, 0, 1, 3, 4)
        part = total(exchange(share, "tl")).astype(BF16)
        part = part.reshape(2, 2, 16, 2, 512).transpose(3, 1, 0, 2, 4).reshape(4, 32, 512)
        part = total(exchange(part, ("zh", "th"))).astype(BF16)
        part = part.reshape(32, 4, 128).transpose(1, 0, 2)
        grad_input = exchange(part, "x").reshape(128, 128)

    with jax.named_scope("grad_columns"):
        grad_cols = jnp.stack([grads[0]] + [shift(grads[k], k) for k in range(1, 4)])

        grad_cols = grad_cols.reshape(1024, 512)

    with jax.named_scope("grad_weight"):
        grad_weight = tn_dot(all_tokens, grad_cols).astype(BF16)

    with jax.named_scope("grad_factor"):
        pieces = both_th(factor_piece, swap(factor_piece, "th"), th)
        pieces = [pieces] + [lax.ppermute(pieces, "tl", ring(k)) for k in range(1, 4)]
        pieces = jnp.stack([pick(pieces, (tl - a) % 4) for a in range(4)], axis=1)
        cross = exchange(pieces.reshape(8, 128, 512), IN).reshape(1024, 512)
        grad_factor = tn_dot(grad_cols, cross) / 1024.0

    with jax.named_scope("act_factor"):
        act_cols = cols_of(all_tokens, x % 2 * 512, 512)
        act_cols = jnp.where(core == x // 2, act_cols, swap(act_cols, "core"))
        from_y = lax.ppermute(act_cols, "y", [(0, 1), (1, 0), (2, 3), (3, 2)])
        act_cols = jnp.where(y % 2 == zh, act_cols, from_y)
        act_factor = tn_dot(cols_of(all_tokens, tok * 128, 128), act_cols) / 1024.0
    return (grad_input, grad_weight, act_factor, grad_factor)


def solution(mesh):
    fine = Mesh(mesh.devices.reshape(4, 2, 2, 4, 2, 4), ("y", "core", "zh", "x", "th", "tl"))
    return jax.shard_map(
        on_device,
        mesh=fine,
        in_specs=(P(TOK, IN), P(IN, OUT + TOK), P(TOK, OUT)),
        out_specs=(P(TOK, IN + OUT), P(IN, OUT + TOK), P(IN + TOK, OUT), P(OUT + TOK, IN)),
        check_vma=False,
    )
```

```python
import math

import jax
import jax.numpy as jnp
from jax import lax
from jax.sharding import Mesh, PartitionSpec as P

BF16 = jnp.bfloat16
F16 = jnp.float16
F32 = jnp.float32
IN = ("y", "core")
OUT = ("zh", "x")
TOK = ("th", "tl")
TOKEN_SCALE = 8192.0
GRAD_SCALE = 4096.0


def gelu_slope(values):
    scale = math.sqrt(2.0 / math.pi)
    cubic = values * values * values
    tanh_val = jnp.tanh(scale * (values + 0.044715 * cubic))
    return 0.5 * (1.0 + tanh_val) + 0.5 * values * (1.0 - tanh_val * tanh_val) * scale * (
        1.0 + 3.0 * 0.044715 * values * values
    )


def swap(value, axis):
    return lax.ppermute(value, axis, [(0, 1), (1, 0)])


def ring(step):
    return [(i, (i + step) % 4) for i in range(4)]


def pick(values, at):
    low = jnp.where(at == 0, values[0], values[1])
    high = jnp.where(at == 2, values[2], values[3])
    return jnp.where(at < 2, low, high)


def exchange(value, axis):
    return lax.all_to_all(value, axis, split_axis=0, concat_axis=0, tiled=True)


def spread(value, axis):
    size = lax.axis_size(axis)
    return exchange(jnp.broadcast_to(value[None], (size,) + value.shape), axis)


def total(parts):
    return jnp.sum(parts.astype(F32), axis=0)


def rows_of(value, start, size):
    return lax.dynamic_slice_in_dim(value, start, size, 0)


def cols_of(value, start, size):
    return lax.dynamic_slice_in_dim(value, start, size, 1)


def both_th(own, other, th):
    return jnp.where(th == 0, jnp.stack([own, other]), jnp.stack([other, own]))


def gather_scaled(value, axis, scale):
    scaled = (value.astype(F32) * scale).astype(F16)
    return lax.all_gather(scaled, axis, axis=0, tiled=True)


def unscaled(value, scale):
    return (value.astype(F32) * (1.0 / scale)).astype(BF16)


def tn_dot(left, right):
    return lax.dot_general(left, right, (((0,), (0,)), ((), ())), preferred_element_type=F32)


def on_device(tokens_in, weight, grad_out):
    y, core, zh, x, th, tl = (lax.axis_index(a) for a in ("y", "core", "zh", "x", "th", "tl"))
    tok = th * 4 + tl
    piece = y * 2 + core

    with jax.named_scope("grad_out_piece"):
        grad_out_rows = lax.all_gather(rows_of(grad_out, piece * 16, 16), TOK, axis=0, tiled=True)

    with jax.named_scope("gather_tokens"):
        own = rows_of(tokens_in, x * 32, 32)
        near = spread(both_th(own, swap(own, "th"), th), "tl")
        near = near.reshape(4, 2, 2, 16, 1024).transpose(2, 1, 0, 3, 4).reshape(256, 1024)
        tokens = unscaled(gather_scaled(near, "x", TOKEN_SCALE), TOKEN_SCALE)

    with jax.named_scope("preact"):
        partial = jnp.dot(tokens, weight, preferred_element_type=F32).astype(F16)
        preact = total(exchange(partial.reshape(8, 128, 512), IN))
        grad_out_piece = cols_of(grad_out_rows, tok * 512, 512)
        grad_piece = (grad_out_piece.astype(F32) * gelu_slope(preact)).astype(BF16)

    with jax.named_scope("gather_grad"):
        grad_rows = gather_scaled(grad_piece, IN, GRAD_SCALE)
        grad_rows, other_piece = lax.optimization_barrier((grad_rows, swap(grad_piece, "th")))
        grad_rows = unscaled(grad_rows, GRAD_SCALE)

    with jax.named_scope("gather_factor"):
        pieces = both_th(grad_piece, other_piece, th)
        pieces = [pieces] + [lax.ppermute(pieces, "tl", ring(k)) for k in range(1, 4)]

    with jax.named_scope("act_columns"):
        act_cols = cols_of(tokens, x % 2 * 512, 512)
        act_cols = jnp.where(core == x // 2, act_cols, swap(act_cols, "core"))
        from_y = lax.ppermute(act_cols, "y", [(0, 1), (1, 0), (2, 3), (3, 2)])

    with jax.named_scope("grad_input"):
        by_x = weight.reshape(2, 4, 128, 512).transpose(1, 0, 2, 3).reshape(4, 256, 512)
        share = jnp.einsum("rc,kfc->krf", grad_rows, by_x, preferred_element_type=F32).astype(BF16)
        part, pieces = lax.optimization_barrier((exchange(share, "x"), pieces))
        part = total(part).astype(BF16).reshape(8, 2, 4, 16, 256).transpose(2, 0, 1, 3, 4)
        part, from_y = lax.optimization_barrier((exchange(part, "tl"), from_y))
        part = total(part).astype(BF16)
        part = part.reshape(8, 2, 16, 2, 128).transpose(3, 1, 0, 2, 4).reshape(4, 128, 128)
        grad_input = total(exchange(part, ("zh", "th"))).astype(BF16)

    with jax.named_scope("grad_weight"):
        grad_weight = tn_dot(tokens, grad_rows).astype(BF16)

    with jax.named_scope("grad_factor"):
        pieces = jnp.stack([pick(pieces, (tl - a) % 4) for a in range(4)], axis=1)
        cross = exchange(pieces.reshape(8, 128, 512), IN).reshape(1024, 512)
        grad_factor = tn_dot(grad_rows, cross) / 1024.0

    with jax.named_scope("act_factor"):
        act_cols = jnp.where(y % 2 == zh, act_cols, from_y)
        act_factor = tn_dot(cols_of(tokens, tok * 128, 128), act_cols) / 1024.0
    return (grad_input, grad_weight, act_factor, grad_factor)


def solution(mesh):
    fine = Mesh(mesh.devices.reshape(4, 2, 2, 4, 2, 4), ("y", "core", "zh", "x", "th", "tl"))
    return jax.shard_map(
        on_device,
        mesh=fine,
        in_specs=(P(TOK, IN), P(IN, OUT + TOK), P(TOK, OUT)),
        out_specs=(P(TOK, IN + OUT), P(IN, OUT + TOK), P(IN + TOK, OUT), P(OUT + TOK, IN)),
        check_vma=False,
    )
```

```python
import math

import jax
import jax.numpy as jnp
from jax import lax
from jax.sharding import Mesh, PartitionSpec as P

BF16 = jnp.bfloat16
F16 = jnp.float16
F32 = jnp.float32
IN = ("y", "core")
OUT = ("zh", "x")
TOK = ("th", "tl")
TOKEN_SCALE = 8192.0
GRAD_SCALE = 4096.0


def gelu_slope(values):
    scale = math.sqrt(2.0 / math.pi)
    cubic = values * values * values
    tanh_val = jnp.tanh(scale * (values + 0.044715 * cubic))
    return 0.5 * (1.0 + tanh_val) + 0.5 * values * (1.0 - tanh_val * tanh_val) * scale * (
        1.0 + 3.0 * 0.044715 * values * values
    )


def swap(value, axis):
    return lax.ppermute(value, axis, [(0, 1), (1, 0)])


def send_along(value, bit, holders):
    pairs = [(i * 8 + (i ^ h), i * 8 + (i ^ h ^ bit)) for i in range(8) for h in holders]
    return lax.ppermute(value, IN + TOK, pairs)


def exchange(value, axis):
    return lax.all_to_all(value, axis, split_axis=0, concat_axis=0, tiled=True)


def spread(value, axis):
    size = lax.axis_size(axis)
    return exchange(jnp.broadcast_to(value[None], (size,) + value.shape), axis)


def total(parts):
    return jnp.sum(parts.astype(F32), axis=0)


def rows_of(value, start, size):
    return lax.dynamic_slice_in_dim(value, start, size, 0)


def cols_of(value, start, size):
    return lax.dynamic_slice_in_dim(value, start, size, 1)


def gather_scaled(value, axis, scale):
    scaled = (value.astype(F32) * scale).astype(F16)
    return lax.all_gather(scaled, axis, axis=0, tiled=True)


def unscaled(value, scale):
    return (value.astype(F32) * (1.0 / scale)).astype(BF16)


def tn_dot(left, right):
    return lax.dot_general(left, right, (((0,), (0,)), ((), ())), preferred_element_type=F32)


def on_device(tokens_in, weight, grad_out):
    y, core, zh, x, th, tl = (lax.axis_index(a) for a in ("y", "core", "zh", "x", "th", "tl"))
    tok = th * 4 + tl
    piece = y * 2 + core

    with jax.named_scope("grad_out_piece"):
        own_grad, own = lax.optimization_barrier(
            (rows_of(grad_out, piece * 16, 16), rows_of(tokens_in, x * 32, 32))
        )
        grad_out_rows = lax.all_gather(own_grad, TOK, axis=0, tiled=True)

    with jax.named_scope("gather_tokens"):
        near = spread(own, TOK).reshape(8, 2, 16, 1024)
        near = near.transpose(1, 0, 2, 3).reshape(256, 1024)
        tokens = unscaled(gather_scaled(near, "x", TOKEN_SCALE), TOKEN_SCALE)

    with jax.named_scope("preact"):
        partial = jnp.dot(tokens, weight, preferred_element_type=F32).astype(F16)
        preact = total(exchange(partial.reshape(8, 128, 512), IN))
        grad_out_piece = cols_of(grad_out_rows, tok * 512, 512)
        grad_piece = (grad_out_piece.astype(F32) * gelu_slope(preact)).astype(BF16)

    with jax.named_scope("gather_grad"):
        grad_rows = unscaled(gather_scaled(grad_piece, IN, GRAD_SCALE), GRAD_SCALE)

    with jax.named_scope("factor_columns"):
        away = tok ^ piece
        far = send_along(grad_rows, 4, (0,))
        cross = jnp.where(away == 0, grad_rows, far)
        mid = send_along(cross, 2, (0, 4))
        cross = jnp.where(away & 2 == 0, cross, mid)

    with jax.named_scope("act_columns"):
        act_cols = cols_of(tokens, x % 2 * 512, 512)
        act_cols = jnp.where(core == x // 2, act_cols, swap(act_cols, "core"))
        from_y = lax.ppermute(act_cols, "y", [(0, 1), (1, 0), (2, 3), (3, 2)])

    with jax.named_scope("grad_input"):
        by_x = weight.reshape(2, 4, 128, 512).transpose(1, 0, 2, 3).reshape(4, 256, 512)
        share = jnp.einsum("rc,kfc->krf", grad_rows, by_x, preferred_element_type=F32).astype(BF16)
        part, far = lax.optimization_barrier((exchange(share, "x"), far))
        part = total(part).astype(BF16).reshape(8, 2, 4, 16, 256).transpose(2, 0, 1, 3, 4)
        part = total(exchange(part, "tl")).astype(BF16)
        part = part.reshape(8, 2, 16, 2, 128).transpose(3, 1, 0, 2, 4).reshape(4, 128, 128)
        part, cross, from_y = lax.optimization_barrier((part, cross, from_y))
        grad_input = total(exchange(part, ("zh", "th"))).astype(BF16)

    with jax.named_scope("grad_weight"):
        grad_weight = tn_dot(tokens, grad_rows).astype(BF16)

    with jax.named_scope("grad_factor"):
        near = send_along(cross, 1, (0, 2, 4, 6))
        cross = jnp.where(away & 1 == 0, cross, near)
        grad_factor = tn_dot(grad_rows, cross) / 1024.0

    with jax.named_scope("act_factor"):
        act_cols = jnp.where(y % 2 == zh, act_cols, from_y)
        act_factor = tn_dot(cols_of(tokens, tok * 128, 128), act_cols) / 1024.0
    return (grad_input, grad_weight, act_factor, grad_factor)


def solution(mesh):
    fine = Mesh(mesh.devices.reshape(4, 2, 2, 4, 2, 4), ("y", "core", "zh", "x", "th", "tl"))
    return jax.shard_map(
        on_device,
        mesh=fine,
        in_specs=(P(TOK, IN), P(IN, OUT + TOK), P(TOK, OUT)),
        out_specs=(P(TOK, IN + OUT), P(IN, OUT + TOK), P(IN + TOK, OUT), P(OUT + TOK, IN)),
        check_vma=False,
    )
```

```python
import math

import jax
import jax.numpy as jnp
from jax import lax
from jax.sharding import Mesh, PartitionSpec as P

BF16 = jnp.bfloat16
F16 = jnp.float16
F32 = jnp.float32
IN = ("y", "core")
OUT = ("zh", "x")
TOK = ("th", "tl")
TOKEN_SCALE = 8192.0
GRAD_SCALE = 4096.0


def gelu_slope(values):
    scale = math.sqrt(2.0 / math.pi)
    cubic = values * values * values
    tanh_val = jnp.tanh(scale * (values + 0.044715 * cubic))
    return 0.5 * (1.0 + tanh_val) + 0.5 * values * (1.0 - tanh_val * tanh_val) * scale * (
        1.0 + 3.0 * 0.044715 * values * values
    )


def swap(value, axis):
    return lax.ppermute(value, axis, [(0, 1), (1, 0)])


def send_along(value, bit, holders):
    pairs = [(i * 8 + (i ^ h), i * 8 + (i ^ h ^ bit)) for i in range(8) for h in holders]
    return lax.ppermute(value, IN + TOK, pairs)


def exchange(value, axis):
    return lax.all_to_all(value, axis, split_axis=0, concat_axis=0, tiled=True)


def spread(value, axis):
    size = lax.axis_size(axis)
    return exchange(jnp.broadcast_to(value[None], (size,) + value.shape), axis)


def total(parts):
    return jnp.sum(parts.astype(F32), axis=0)


def rows_of(value, start, size):
    return lax.dynamic_slice_in_dim(value, start, size, 0)


def cols_of(value, start, size):
    return lax.dynamic_slice_in_dim(value, start, size, 1)


def gather_scaled(value, axis, scale):
    scaled = (value.astype(F32) * scale).astype(F16)
    return lax.all_gather(scaled, axis, axis=0, tiled=True)


def unscaled(value, scale):
    return (value.astype(F32) * (1.0 / scale)).astype(BF16)


def tn_dot(left, right):
    return lax.dot_general(left, right, (((0,), (0,)), ((), ())), preferred_element_type=F32)


def on_device(tokens_in, weight, grad_out):
    y, core, zh, x, th, tl = (lax.axis_index(a) for a in ("y", "core", "zh", "x", "th", "tl"))
    tok = th * 4 + tl
    piece = y * 2 + core

    with jax.named_scope("grad_out_piece"):
        own_grad, own = lax.optimization_barrier(
            (rows_of(grad_out, piece * 16, 16), rows_of(tokens_in, x * 32, 32))
        )
        grad_out_rows = lax.all_gather(own_grad, TOK, axis=0, tiled=True)

    with jax.named_scope("gather_tokens"):
        other = swap(own, "th")
        near = jnp.where(th == 0, jnp.stack([own, other]), jnp.stack([other, own]))
        near = spread(near, "tl").reshape(4, 2, 2, 16, 1024).transpose(2, 1, 0, 3, 4)
        near = near.reshape(256, 1024)
        tokens = unscaled(gather_scaled(near, "x", TOKEN_SCALE), TOKEN_SCALE)

    with jax.named_scope("preact"):
        partial = jnp.dot(tokens, weight, preferred_element_type=F32).astype(F16)
        act_cols = cols_of(tokens, x % 2 * 512, 512)
        act_other = swap(act_cols, "core")
        parts, act_other = lax.optimization_barrier(
            (exchange(partial.reshape(8, 128, 512), IN), act_other)
        )
        preact = total(parts)
        grad_out_piece = cols_of(grad_out_rows, tok * 512, 512)
        grad_piece = (grad_out_piece.astype(F32) * gelu_slope(preact)).astype(BF16)

    with jax.named_scope("gather_grad"):
        grad_rows = unscaled(gather_scaled(grad_piece, IN, GRAD_SCALE), GRAD_SCALE)

    with jax.named_scope("factor_columns"):
        away = tok ^ piece
        far = send_along(grad_rows, 4, (0,))
        cross = jnp.where(away == 0, grad_rows, far)
        mid = send_along(cross, 2, (0, 4))

    with jax.named_scope("act_columns"):
        act_cols = jnp.where(core == x // 2, act_cols, act_other)
        from_y = lax.ppermute(act_cols, "y", [(0, 1), (1, 0), (2, 3), (3, 2)])

    with jax.named_scope("grad_input"):
        by_x = weight.reshape(2, 4, 128, 512).transpose(1, 0, 2, 3).reshape(4, 256, 512)
        share = jnp.einsum("rc,kfc->krf", grad_rows, by_x, preferred_element_type=F32).astype(BF16)
        part, far, from_y = lax.optimization_barrier((exchange(share, "x"), far, from_y))
        part = total(part).astype(BF16).reshape(8, 8, 16, 256).transpose(1, 0, 2, 3)
        part, mid = lax.optimization_barrier((exchange(part, TOK), mid))
        part = total(part).reshape(128, 256)
        keep = jnp.where(zh == 0, part[:, :128], part[:, 128:])
        send = jnp.where(zh == 0, part[:, 128:], part[:, :128]).astype(BF16)
        grad_input = (keep + swap(send, "zh").astype(F32)).astype(BF16)

    with jax.named_scope("grad_weight"):
        grad_weight = tn_dot(tokens, grad_rows).astype(BF16)

    with jax.named_scope("grad_factor"):
        cross = jnp.where(away & 2 == 0, cross, mid)
        near = send_along(cross, 1, (0, 2, 4, 6))
        cross = jnp.where(away & 1 == 0, cross, near)
        grad_factor = tn_dot(grad_rows, cross) / 1024.0

    with jax.named_scope("act_factor"):
        act_cols = jnp.where(y % 2 == zh, act_cols, from_y)
        act_factor = tn_dot(cols_of(tokens, tok * 128, 128), act_cols) / 1024.0
    return (grad_input, grad_weight, act_factor, grad_factor)


def solution(mesh):
    fine = Mesh(mesh.devices.reshape(4, 2, 2, 4, 2, 4), ("y", "core", "zh", "x", "th", "tl"))
    return jax.shard_map(
        on_device,
        mesh=fine,
        in_specs=(P(TOK, IN), P(IN, OUT + TOK), P(TOK, OUT)),
        out_specs=(P(TOK, IN + OUT), P(IN, OUT + TOK), P(IN + TOK, OUT), P(OUT + TOK, IN)),
        check_vma=False,
    )
```

```python
import math

import jax
import jax.numpy as jnp
from jax import lax
from jax.sharding import Mesh, PartitionSpec as P

BF16 = jnp.bfloat16
F16 = jnp.float16
F32 = jnp.float32
IN = ("y", "core")
OUT = ("zh", "x")
TOK = ("th", "tl")
TOKEN_SCALE = 8192.0
GRAD_SCALE = 4096.0


def gelu_slope(values):
    scale = math.sqrt(2.0 / math.pi)
    cubic = values * values * values
    tanh_val = jnp.tanh(scale * (values + 0.044715 * cubic))
    return 0.5 * (1.0 + tanh_val) + 0.5 * values * (1.0 - tanh_val * tanh_val) * scale * (
        1.0 + 3.0 * 0.044715 * values * values
    )


def swap(value, axis):
    return lax.ppermute(value, axis, [(0, 1), (1, 0)])


def send_along(value, bit, holders):
    pairs = [(i * 8 + (i ^ h), i * 8 + (i ^ h ^ bit)) for i in range(8) for h in holders]
    return lax.ppermute(value, IN + TOK, pairs)


def exchange(value, axis):
    return lax.all_to_all(value, axis, split_axis=0, concat_axis=0, tiled=True)


def spread(value, axis):
    size = lax.axis_size(axis)
    return exchange(jnp.broadcast_to(value[None], (size,) + value.shape), axis)


def total(parts):
    return jnp.sum(parts.astype(F32), axis=0)


def rows_of(value, start, size):
    return lax.dynamic_slice_in_dim(value, start, size, 0)


def cols_of(value, start, size):
    return lax.dynamic_slice_in_dim(value, start, size, 1)


def gather_scaled(value, axis, scale):
    scaled = (value.astype(F32) * scale).astype(F16)
    return lax.all_gather(scaled, axis, axis=0, tiled=True)


def unscaled(value, scale):
    return (value.astype(F32) * (1.0 / scale)).astype(BF16)


def tn_dot(left, right):
    return lax.dot_general(left, right, (((0,), (0,)), ((), ())), preferred_element_type=F32)


def on_device(tokens_in, weight, grad_out):
    y, core, zh, x, th, tl = (lax.axis_index(a) for a in ("y", "core", "zh", "x", "th", "tl"))
    tok = th * 4 + tl
    piece = y * 2 + core

    with jax.named_scope("grad_out_piece"):
        own_grad, own = lax.optimization_barrier(
            (rows_of(grad_out, piece * 16, 16), rows_of(tokens_in, x * 32, 32))
        )
        grad_out_rows = lax.all_gather(own_grad, TOK, axis=0, tiled=True)

    with jax.named_scope("gather_tokens"):
        near = spread(own, TOK).reshape(8, 2, 16, 1024)
        near = near.transpose(1, 0, 2, 3).reshape(256, 1024)
        tokens = unscaled(gather_scaled(near, "x", TOKEN_SCALE), TOKEN_SCALE)

    with jax.named_scope("preact"):
        partial = jnp.dot(tokens, weight, preferred_element_type=F32).astype(F16)
        act_cols = cols_of(tokens, x % 2 * 512, 512)
        act_other = swap(act_cols, "core")
        parts, act_other = lax.optimization_barrier(
            (exchange(partial.reshape(8, 128, 512), IN), act_other)
        )
        preact = total(parts)
        grad_out_piece = cols_of(grad_out_rows, tok * 512, 512)
        grad_piece = (grad_out_piece.astype(F32) * gelu_slope(preact)).astype(BF16)

    with jax.named_scope("gather_grad"):
        grad_rows = unscaled(gather_scaled(grad_piece, IN, GRAD_SCALE), GRAD_SCALE)

    with jax.named_scope("factor_columns"):
        away = tok ^ piece
        far = send_along(grad_rows, 4, (0,))
        cross = jnp.where(away == 0, grad_rows, far)

    with jax.named_scope("act_columns"):
        act_cols = jnp.where(core == x // 2, act_cols, act_other)
        from_y = lax.ppermute(act_cols, "y", [(0, 1), (1, 0), (2, 3), (3, 2)])

    with jax.named_scope("grad_input"):
        by_x = weight.reshape(2, 4, 128, 512).transpose(1, 0, 2, 3).reshape(4, 256, 512)
        share = jnp.einsum("rc,kfc->krf", grad_rows, by_x, preferred_element_type=F32).astype(BF16)
        part, cross = lax.optimization_barrier((exchange(share, "x"), cross))
        mid = send_along(cross, 2, (0, 4))
        part = total(part).astype(BF16).reshape(8, 2, 4, 16, 256).transpose(2, 0, 1, 3, 4)
        part, from_y, mid = lax.optimization_barrier((exchange(part, "tl"), from_y, mid))
        part = total(part).astype(BF16)
        part = part.reshape(8, 2, 16, 2, 128).transpose(3, 1, 0, 2, 4).reshape(4, 128, 128)
        grad_input = total(exchange(part, ("zh", "th"))).astype(BF16)

    with jax.named_scope("grad_weight"):
        grad_weight = tn_dot(tokens, grad_rows).astype(BF16)

    with jax.named_scope("grad_factor"):
        cross = jnp.where(away & 2 == 0, cross, mid)
        near = send_along(cross, 1, (0, 2, 4, 6))
        cross = jnp.where(away & 1 == 0, cross, near)
        grad_factor = tn_dot(grad_rows, cross) / 1024.0

    with jax.named_scope("act_factor"):
        act_cols = jnp.where(y % 2 == zh, act_cols, from_y)
        act_factor = tn_dot(cols_of(tokens, tok * 128, 128), act_cols) / 1024.0
    return (grad_input, grad_weight, act_factor, grad_factor)


def solution(mesh):
    fine = Mesh(mesh.devices.reshape(4, 2, 2, 4, 2, 4), ("y", "core", "zh", "x", "th", "tl"))
    return jax.shard_map(
        on_device,
        mesh=fine,
        in_specs=(P(TOK, IN), P(IN, OUT + TOK), P(TOK, OUT)),
        out_specs=(P(TOK, IN + OUT), P(IN, OUT + TOK), P(IN + TOK, OUT), P(OUT + TOK, IN)),
        check_vma=False,
    )
```

```python
import math

import jax
import jax.numpy as jnp
from jax import lax
from jax.experimental import pallas as pl
from jax.experimental.pallas import tpu as pltpu
from jax.sharding import Mesh, PartitionSpec as P

BF16 = jnp.bfloat16
F16 = jnp.float16
F32 = jnp.float32
IN = ("yh", "yl", "core")
OUT = ("zh", "x")
TOK = ("th", "tl")
TOKEN_SCALE = 8192.0
GRAD_SCALE = 4096.0


def gelu_slope(values):
    scale = math.sqrt(2.0 / math.pi)
    cubic = values * values * values
    tanh_val = jnp.tanh(scale * (values + 0.044715 * cubic))
    return 0.5 * (1.0 + tanh_val) + 0.5 * values * (1.0 - tanh_val * tanh_val) * scale * (
        1.0 + 3.0 * 0.044715 * values * values
    )


def swap(value, axis):
    return lax.ppermute(value, axis, [(0, 1), (1, 0)])


def send_along(value, bit, holders):
    pairs = [(i * 8 + (i ^ h), i * 8 + (i ^ h ^ bit)) for i in range(8) for h in holders]
    return lax.ppermute(value, IN + TOK, pairs)


def exchange(value, axis):
    return lax.all_to_all(value, axis, split_axis=0, concat_axis=0, tiled=True)


def spread(value, axis):
    size = lax.axis_size(axis)
    return exchange(jnp.broadcast_to(value[None], (size,) + value.shape), axis)


def total(parts):
    return jnp.sum(parts.astype(F32), axis=0)


def rows_of(value, start, size):
    return lax.dynamic_slice_in_dim(value, start, size, 0)


def cols_of(value, start, size):
    return lax.dynamic_slice_in_dim(value, start, size, 1)


def gather_scaled(value, axis, scale):
    scaled = (value.astype(F32) * scale).astype(F16)
    return lax.all_gather(scaled, axis, axis=0, tiled=True)


def unscaled(value, scale):
    return (value.astype(F32) * (1.0 / scale)).astype(BF16)


def tn_dot(left, right):
    return lax.dot_general(left, right, (((0,), (0,)), ((), ())), preferred_element_type=F32)


def sum_kernel(parts_ref, out_ref):
    out_ref[0] = jnp.sum(parts_ref[:, :, 0].astype(F32), axis=0).astype(BF16)


def sum_by_tl(parts):
    return pl.pallas_call(
        sum_kernel,
        grid=(4,),
        in_specs=[pl.BlockSpec((4, 16, 1, 16, 256), lambda i: (0, 0, i, 0, 0))],
        out_specs=pl.BlockSpec((1, 16, 16, 256), lambda i: (i, 0, 0, 0)),
        out_shape=jax.ShapeDtypeStruct((4, 16, 16, 256), BF16),
        compiler_params=pltpu.CompilerParams(vmem_limit_bytes=16 * 2**20),
        cost_estimate=pl.CostEstimate(flops=2**20, bytes_accessed=5 * 2**19, transcendentals=0),
    )(parts.reshape(4, 16, 4, 16, 256))


def on_device(tokens_in, weight, grad_out):
    core, zh, x, th, tl = (lax.axis_index(a) for a in ("core", "zh", "x", "th", "tl"))
    tok = th * 4 + tl
    piece = lax.axis_index(IN)

    with jax.named_scope("grad_out_piece"):
        own_grad, own = lax.optimization_barrier(
            (rows_of(grad_out, piece * 16, 16), rows_of(tokens_in, x * 32, 32))
        )
        grad_out_rows = lax.all_gather(own_grad, TOK, axis=0, tiled=True)

    with jax.named_scope("gather_tokens"):
        near = spread(own, TOK).reshape(8, 2, 16, 1024)
        near = near.transpose(1, 0, 2, 3).reshape(256, 1024)
        tokens = unscaled(gather_scaled(near, "x", TOKEN_SCALE), TOKEN_SCALE)

    with jax.named_scope("preact"):
        partial = jnp.dot(tokens, weight, preferred_element_type=F32).astype(F16)
        act_cols = cols_of(tokens, x % 2 * 512, 512)
        act_other = swap(act_cols, "core")
        parts, act_other = lax.optimization_barrier(
            (exchange(partial.reshape(8, 128, 512), IN), act_other)
        )
        preact = total(parts)
        grad_out_piece = cols_of(grad_out_rows, tok * 512, 512)
        grad_piece = (grad_out_piece.astype(F32) * gelu_slope(preact)).astype(BF16)

    with jax.named_scope("gather_grad"):
        grad_rows = unscaled(gather_scaled(grad_piece, IN, GRAD_SCALE), GRAD_SCALE)

    with jax.named_scope("factor_columns"):
        away = tok ^ piece
        far = send_along(grad_rows, 4, (0,))
        cross = jnp.where(away == 0, grad_rows, far)

    with jax.named_scope("act_columns"):
        act_cols = jnp.where(core == x // 2, act_cols, act_other)
        act_pair = lax.all_gather(act_cols, "yl", axis=0)

    with jax.named_scope("grad_input"):
        by_x = weight.reshape(2, 4, 128, 512).transpose(1, 0, 2, 3).reshape(4, 256, 512)
        share = jnp.einsum("rc,kfc->krf", grad_rows, by_x, preferred_element_type=F32).astype(BF16)
        part, cross = lax.optimization_barrier((exchange(share, "x"), cross))
        mid = send_along(cross, 2, (0, 4))
        part, mid = lax.optimization_barrier((exchange(sum_by_tl(part), "tl"), mid))
        part = total(part).astype(BF16)
        part = part.reshape(8, 2, 16, 2, 128).transpose(3, 1, 0, 2, 4).reshape(4, 128, 128)
        grad_input = total(exchange(part, ("zh", "th"))).astype(BF16)

    with jax.named_scope("grad_weight"):
        grad_weight = tn_dot(tokens, grad_rows).astype(BF16)

    with jax.named_scope("grad_factor"):
        cross = jnp.where(away & 2 == 0, cross, mid)
        near = send_along(cross, 1, (0, 2, 4, 6))
        cross = jnp.where(away & 1 == 0, cross, near)
        grad_factor = tn_dot(grad_rows, cross) / 1024.0

    with jax.named_scope("act_factor"):
        act_cols = lax.dynamic_index_in_dim(act_pair, zh, 0, keepdims=False)
        act_factor = tn_dot(cols_of(tokens, tok * 128, 128), act_cols) / 1024.0
    return (grad_input, grad_weight, act_factor, grad_factor)


def solution(mesh):
    fine = Mesh(mesh.devices.reshape(2, 2, 2, 2, 4, 2, 4), IN + OUT + TOK)
    return jax.shard_map(
        on_device,
        mesh=fine,
        in_specs=(P(TOK, IN), P(IN, OUT + TOK), P(TOK, OUT)),
        out_specs=(P(TOK, IN + OUT), P(IN, OUT + TOK), P(IN + TOK, OUT), P(OUT + TOK, IN)),
        check_vma=False,
    )
```

```python
import math

import jax
import jax.numpy as jnp
from jax import lax
from jax.experimental import pallas as pl
from jax.experimental.pallas import tpu as pltpu
from jax.sharding import Mesh, PartitionSpec as P

BF16 = jnp.bfloat16
F16 = jnp.float16
F32 = jnp.float32
IN = ("yh", "yl", "core")
OUT = ("zh", "x")
TOK = ("th", "tl")
TOKEN_SCALE = 8192.0
GRAD_SCALE = 4096.0


def gelu_slope(values):
    scale = math.sqrt(2.0 / math.pi)
    cubic = values * values * values
    tanh_val = jnp.tanh(scale * (values + 0.044715 * cubic))
    return 0.5 * (1.0 + tanh_val) + 0.5 * values * (1.0 - tanh_val * tanh_val) * scale * (
        1.0 + 3.0 * 0.044715 * values * values
    )


def swap(value, axis):
    return lax.ppermute(value, axis, [(0, 1), (1, 0)])


def send_along(value, bit, holders):
    pairs = [(i * 8 + (i ^ h), i * 8 + (i ^ h ^ bit)) for i in range(8) for h in holders]
    return lax.ppermute(value, IN + TOK, pairs)


def exchange(value, axis):
    return lax.all_to_all(value, axis, split_axis=0, concat_axis=0, tiled=True)


def total(parts):
    return jnp.sum(parts.astype(F32), axis=0)


def rows_of(value, start, size):
    return lax.dynamic_slice_in_dim(value, start, size, 0)


def cols_of(value, start, size):
    return lax.dynamic_slice_in_dim(value, start, size, 1)


def both_th(own, other, th):
    return jnp.where(th == 0, jnp.stack([own, other]), jnp.stack([other, own]))


def gather_scaled(value, axis, scale):
    scaled = (value.astype(F32) * scale).astype(F16)
    return lax.all_gather(scaled, axis, axis=0, tiled=True)


def unscaled(value, scale):
    return (value.astype(F32) * (1.0 / scale)).astype(BF16)


def tn_dot(left, right):
    return lax.dot_general(left, right, (((0,), (0,)), ((), ())), preferred_element_type=F32)


def sum_kernel(parts_ref, out_ref):
    out_ref[0] = jnp.sum(parts_ref[:, :, 0].astype(F32), axis=0).astype(BF16)


def sum_by_tl(parts):
    return pl.pallas_call(
        sum_kernel,
        grid=(4,),
        in_specs=[pl.BlockSpec((4, 16, 1, 16, 256), lambda i: (0, 0, i, 0, 0))],
        out_specs=pl.BlockSpec((1, 16, 16, 256), lambda i: (i, 0, 0, 0)),
        out_shape=jax.ShapeDtypeStruct((4, 16, 16, 256), BF16),
        compiler_params=pltpu.CompilerParams(vmem_limit_bytes=16 * 2**20),
        cost_estimate=pl.CostEstimate(flops=2**20, bytes_accessed=5 * 2**19, transcendentals=0),
    )(parts.reshape(4, 16, 4, 16, 256))


def split_kernel(parts_ref, out_ref):
    added = jnp.sum(parts_ref[:, :, 0].astype(F32), axis=0).astype(BF16)
    out_ref[0, 0] = added[:, :, :128]
    out_ref[1, 0] = added[:, :, 128:]


def sum_by_zh_th(parts):
    return pl.pallas_call(
        split_kernel,
        grid=(2,),
        in_specs=[pl.BlockSpec((4, 8, 1, 16, 256), lambda i: (0, 0, i, 0, 0))],
        out_specs=pl.BlockSpec((2, 1, 8, 16, 128), lambda i: (0, i, 0, 0, 0)),
        out_shape=jax.ShapeDtypeStruct((2, 2, 8, 16, 128), BF16),
        compiler_params=pltpu.CompilerParams(vmem_limit_bytes=16 * 2**20),
        cost_estimate=pl.CostEstimate(flops=2**18, bytes_accessed=5 * 2**17, transcendentals=0),
    )(parts.reshape(4, 8, 2, 16, 256)).reshape(4, 128, 128)


def on_device(tokens_in, weight, grad_out):
    core, yl, zh, x, th, tl = (lax.axis_index(a) for a in ("core", "yl", "zh", "x", "th", "tl"))
    tok = th * 4 + tl
    piece = lax.axis_index(IN)

    with jax.named_scope("gather_quarter"):
        own = rows_of(tokens_in, x * 32, 32)
        own_grad = rows_of(grad_out, piece * 16, 16)
        keep = cols_of(own_grad, th * 2048, 2048).reshape(16, 4, 512)
        send = cols_of(own_grad, (1 - th) * 2048, 2048)
        send = jnp.concatenate([own, send[:, :1024], send[:, 1024:]], axis=0)
        got = swap(send, "th")
        got_grad = jnp.concatenate([got[32:48], got[48:]], axis=1).reshape(16, 4, 512)
        near_grad = both_th(keep, got_grad, th).transpose(2, 1, 0, 3).reshape(4, 16, 1024)
        near = both_th(own, got[:32], th).reshape(64, 1024)
        near = jnp.concatenate([jnp.broadcast_to(near[None], (4, 64, 1024)), near_grad], axis=1)
        near = exchange(near, "tl")
        quarter = near[:, :64].reshape(4, 2, 2, 16, 1024).transpose(2, 1, 0, 3, 4)
        grad_out_piece = near[:, 64:].reshape(4, 16, 2, 512).transpose(2, 0, 1, 3).reshape(128, 512)

    with jax.named_scope("gather_tokens"):
        quarter = quarter.reshape(256, 1024)
        tokens = unscaled(gather_scaled(quarter, "x", TOKEN_SCALE), TOKEN_SCALE)

    with jax.named_scope("act_columns"):
        act_start = x % 2 * 512
        act_own = lax.dynamic_slice(tokens, (core * 512, act_start), (512, 512))
        act_other = swap(lax.dynamic_slice(tokens, ((1 - core) * 512, act_start), (512, 512)), "core")

    with jax.named_scope("preact"):
        partial = jnp.dot(tokens, weight, preferred_element_type=F32).astype(F16)
        parts, act_other = lax.optimization_barrier(
            (exchange(partial.reshape(8, 128, 512), IN), act_other)
        )
        preact = total(parts)
        grad_piece = (grad_out_piece.astype(F32) * gelu_slope(preact)).astype(BF16)

    with jax.named_scope("gather_grad"):
        grad_rows = unscaled(gather_scaled(grad_piece, IN, GRAD_SCALE), GRAD_SCALE)

    with jax.named_scope("factor_columns"):
        away = tok ^ piece
        far = send_along(grad_rows, 4, (0,))
        cross = jnp.where(away == 0, grad_rows, far)

    with jax.named_scope("act_columns"):
        act_half = jnp.where(core == x // 2, act_own, act_other)
        from_y = swap(act_half, "yl")

    with jax.named_scope("grad_input"):
        by_x = weight.reshape(2, 4, 128, 512).transpose(1, 0, 2, 3).reshape(4, 256, 512)
        share = jnp.einsum("rc,kfc->krf", grad_rows, by_x, preferred_element_type=F32).astype(BF16)
        part, cross, from_y = lax.optimization_barrier((exchange(share, "x"), cross, from_y))
        mid = send_along(cross, 2, (0, 4))
        part, mid = lax.optimization_barrier((sum_by_tl(part), mid))
        cross = jnp.where(away & 2 == 0, cross, mid)
        near = send_along(cross, 1, (0, 2, 4, 6))
        act_half = jnp.where(yl == zh, act_half, from_y)
        act_rest = swap(act_half, "core")
        part, near = lax.optimization_barrier((exchange(part, "tl"), near))
        part = exchange(sum_by_zh_th(part), ("zh", "th"))
        grad_input = total(part).astype(BF16)

    with jax.named_scope("grad_weight"):
        grad_weight = tn_dot(tokens, grad_rows).astype(BF16)

    with jax.named_scope("grad_factor"):
        cross = jnp.where(away & 1 == 0, cross, near)
        grad_factor = tn_dot(grad_rows, cross) / 1024.0

    with jax.named_scope("act_factor"):
        act_rows = cols_of(tokens, tok * 128, 128)
        act_factor = tn_dot(rows_of(act_rows, core * 512, 512), act_half)
        act_factor += tn_dot(rows_of(act_rows, (1 - core) * 512, 512), act_rest)
        act_factor /= 1024.0
    return (grad_input, grad_weight, act_factor, grad_factor)


def solution(mesh):
    fine = Mesh(mesh.devices.reshape(2, 2, 2, 2, 4, 2, 4), IN + OUT + TOK)
    return jax.shard_map(
        on_device,
        mesh=fine,
        in_specs=(P(TOK, IN), P(IN, OUT + TOK), P(TOK, OUT)),
        out_specs=(P(TOK, IN + OUT), P(IN, OUT + TOK), P(IN + TOK, OUT), P(OUT + TOK, IN)),
        check_vma=False,
    )
```

```python
import math

import jax
import jax.numpy as jnp
from jax import lax
from jax.experimental import pallas as pl
from jax.experimental.pallas import tpu as pltpu
from jax.sharding import Mesh, PartitionSpec as P

BF16 = jnp.bfloat16
F16 = jnp.float16
F32 = jnp.float32
IN = ("yh", "yl", "core")
OUT = ("zh", "x")
TOK = ("th", "tl")
TOKEN_SCALE = 8192.0
GRAD_SCALE = 4096.0


def gelu_slope(values):
    scale = math.sqrt(2.0 / math.pi)
    cubic = values * values * values
    tanh_val = jnp.tanh(scale * (values + 0.044715 * cubic))
    return 0.5 * (1.0 + tanh_val) + 0.5 * values * (1.0 - tanh_val * tanh_val) * scale * (
        1.0 + 3.0 * 0.044715 * values * values
    )


def swap(value, axis):
    return lax.ppermute(value, axis, [(0, 1), (1, 0)])


def send_along(value, bit, holders):
    pairs = [(i * 8 + (i ^ h), i * 8 + (i ^ h ^ bit)) for i in range(8) for h in holders]
    return lax.ppermute(value, IN + TOK, pairs)


def exchange(value, axis):
    return lax.all_to_all(value, axis, split_axis=0, concat_axis=0, tiled=True)


def total(parts):
    return jnp.sum(parts.astype(F32), axis=0)


def rows_of(value, start, size):
    return lax.dynamic_slice_in_dim(value, start, size, 0)


def cols_of(value, start, size):
    return lax.dynamic_slice_in_dim(value, start, size, 1)


def both_th(own, other, th):
    return jnp.where(th == 0, jnp.stack([own, other]), jnp.stack([other, own]))


def gather_scaled(value, axis, scale):
    scaled = (value.astype(F32) * scale).astype(F16)
    return lax.all_gather(scaled, axis, axis=0, tiled=True)


def unscaled(value, scale):
    return (value.astype(F32) * (1.0 / scale)).astype(BF16)


def tn_dot(left, right):
    return lax.dot_general(left, right, (((0,), (0,)), ((), ())), preferred_element_type=F32)


def sum_kernel(parts_ref, out_ref):
    out_ref[0] = jnp.sum(parts_ref[:, :, 0].astype(F32), axis=0).astype(BF16)


def sum_by_tl(parts):
    return pl.pallas_call(
        sum_kernel,
        grid=(4,),
        in_specs=[pl.BlockSpec((4, 16, 1, 16, 256), lambda i: (0, 0, i, 0, 0))],
        out_specs=pl.BlockSpec((1, 16, 16, 256), lambda i: (i, 0, 0, 0)),
        out_shape=jax.ShapeDtypeStruct((4, 16, 16, 256), BF16),
        compiler_params=pltpu.CompilerParams(vmem_limit_bytes=16 * 2**20),
        cost_estimate=pl.CostEstimate(flops=2**20, bytes_accessed=5 * 2**19, transcendentals=0),
    )(parts.reshape(4, 16, 4, 16, 256))


def split_kernel(parts_ref, out_ref):
    added = jnp.sum(parts_ref[:, :, 0].astype(F32), axis=0).astype(BF16)
    out_ref[0, 0] = added[:, :, :128]
    out_ref[1, 0] = added[:, :, 128:]


def sum_by_zh_th(parts):
    return pl.pallas_call(
        split_kernel,
        grid=(2,),
        in_specs=[pl.BlockSpec((4, 8, 1, 16, 256), lambda i: (0, 0, i, 0, 0))],
        out_specs=pl.BlockSpec((2, 1, 8, 16, 128), lambda i: (0, i, 0, 0, 0)),
        out_shape=jax.ShapeDtypeStruct((2, 2, 8, 16, 128), BF16),
        compiler_params=pltpu.CompilerParams(vmem_limit_bytes=16 * 2**20),
        cost_estimate=pl.CostEstimate(flops=2**18, bytes_accessed=5 * 2**17, transcendentals=0),
    )(parts.reshape(4, 8, 2, 16, 256)).reshape(4, 128, 128)


def on_device(tokens_in, weight, grad_out):
    core, yl, zh, x, th, tl = (lax.axis_index(a) for a in ("core", "yl", "zh", "x", "th", "tl"))
    tok = th * 4 + tl
    piece = lax.axis_index(IN)

    with jax.named_scope("gather_quarter"):
        own = rows_of(tokens_in, x * 32, 32)
        own_grad = rows_of(grad_out, piece * 16, 16)
        keep = cols_of(own_grad, th * 2048, 2048).reshape(16, 4, 512)
        send = cols_of(own_grad, (1 - th) * 2048, 2048)
        send = jnp.concatenate([own, send[:, :1024], send[:, 1024:]], axis=0)
        got = swap(send, "th")
        got_grad = jnp.concatenate([got[32:48], got[48:]], axis=1).reshape(16, 4, 512)
        near_grad = both_th(keep, got_grad, th).transpose(2, 1, 0, 3).reshape(4, 16, 1024)
        near = both_th(own, got[:32], th).reshape(64, 1024)
        near = jnp.concatenate([jnp.broadcast_to(near[None], (4, 64, 1024)), near_grad], axis=1)
        near = exchange(near, "tl")
        quarter = near[:, :64].reshape(4, 2, 2, 16, 1024).transpose(2, 1, 0, 3, 4)
        grad_out_piece = near[:, 64:].reshape(4, 16, 2, 512).transpose(2, 0, 1, 3).reshape(128, 512)

    with jax.named_scope("gather_tokens"):
        quarter = quarter.reshape(256, 1024)
        tokens = unscaled(gather_scaled(quarter, "x", TOKEN_SCALE), TOKEN_SCALE)

    with jax.named_scope("act_columns"):
        act_start = x % 2 * 512
        act_own = lax.dynamic_slice(tokens, (core * 512, act_start), (512, 512))
        act_other = swap(lax.dynamic_slice(tokens, ((1 - core) * 512, act_start), (512, 512)), "core")

    with jax.named_scope("preact"):
        partial = jnp.dot(tokens, weight, preferred_element_type=F32).astype(F16)
        parts, act_other = lax.optimization_barrier(
            (exchange(partial.reshape(8, 128, 512), IN), act_other)
        )
        preact = total(parts)
        grad_piece = (grad_out_piece.astype(F32) * gelu_slope(preact)).astype(BF16)

    with jax.named_scope("gather_grad"):
        grad_rows = unscaled(gather_scaled(grad_piece, IN, GRAD_SCALE), GRAD_SCALE)

    with jax.named_scope("factor_columns"):
        away = tok ^ piece
        far = send_along(grad_rows, 4, (0,))
        cross = jnp.where(away == 0, grad_rows, far)

    with jax.named_scope("act_columns"):
        act_half = jnp.where(core == x // 2, act_own, act_other)
        from_y = swap(act_half, "yl")

    with jax.named_scope("grad_input"):
        by_x = weight.reshape(2, 4, 128, 512).transpose(1, 0, 2, 3).reshape(4, 256, 512)
        share = jnp.einsum("rc,kfc->krf", grad_rows, by_x, preferred_element_type=F32).astype(BF16)
        part, cross, from_y = lax.optimization_barrier((exchange(share, "x"), cross, from_y))
        mid = send_along(cross, 2, (0, 4))
        part, mid = lax.optimization_barrier((exchange(sum_by_tl(part), "tl"), mid))
        part = exchange(sum_by_zh_th(part), ("zh", "th"))
        grad_input = total(part).astype(BF16)

    with jax.named_scope("grad_weight"):
        grad_weight = tn_dot(tokens, grad_rows).astype(BF16)

    with jax.named_scope("grad_factor"):
        cross = jnp.where(away & 2 == 0, cross, mid)
        near = send_along(cross, 1, (0, 2, 4, 6))
        cross = jnp.where(away & 1 == 0, cross, near)
        grad_factor = tn_dot(grad_rows, cross) / 1024.0

    with jax.named_scope("act_factor"):
        act_half = jnp.where(yl == zh, act_half, from_y)
        act_rest = swap(act_half, "core")
        act_rows = cols_of(tokens, tok * 128, 128)
        act_factor = tn_dot(rows_of(act_rows, core * 512, 512), act_half)
        act_factor += tn_dot(rows_of(act_rows, (1 - core) * 512, 512), act_rest)
        act_factor /= 1024.0
    return (grad_input, grad_weight, act_factor, grad_factor)


def solution(mesh):
    fine = Mesh(mesh.devices.reshape(2, 2, 2, 2, 4, 2, 4), IN + OUT + TOK)
    return jax.shard_map(
        on_device,
        mesh=fine,
        in_specs=(P(TOK, IN), P(IN, OUT + TOK), P(TOK, OUT)),
        out_specs=(P(TOK, IN + OUT), P(IN, OUT + TOK), P(IN + TOK, OUT), P(OUT + TOK, IN)),
        check_vma=False,
    )
```

```python
import math

import jax
import jax.numpy as jnp
from jax import lax
from jax.experimental import pallas as pl
from jax.experimental.pallas import tpu as pltpu
from jax.sharding import Mesh, PartitionSpec as P

BF16 = jnp.bfloat16
F16 = jnp.float16
F32 = jnp.float32
IN = ("yh", "yl", "core")
OUT = ("zh", "x")
TOK = ("th", "tl")
TOKEN_SCALE = 8192.0
GRAD_SCALE = 4096.0


def gelu_slope(values):
    scale = math.sqrt(2.0 / math.pi)
    cubic = values * values * values
    tanh_val = jnp.tanh(scale * (values + 0.044715 * cubic))
    return 0.5 * (1.0 + tanh_val) + 0.5 * values * (1.0 - tanh_val * tanh_val) * scale * (
        1.0 + 3.0 * 0.044715 * values * values
    )


def swap(value, axis):
    return lax.ppermute(value, axis, [(0, 1), (1, 0)])


def send_along(value, bit, holders):
    pairs = [(i * 8 + (i ^ h), i * 8 + (i ^ h ^ bit)) for i in range(8) for h in holders]
    return lax.ppermute(value, IN + TOK, pairs)


def exchange(value, axis):
    return lax.all_to_all(value, axis, split_axis=0, concat_axis=0, tiled=True)


def total(parts):
    return jnp.sum(parts.astype(F32), axis=0)


def rows_of(value, start, size):
    return lax.dynamic_slice_in_dim(value, start, size, 0)


def cols_of(value, start, size):
    return lax.dynamic_slice_in_dim(value, start, size, 1)


def both_th(own, other, th):
    return jnp.where(th == 0, jnp.stack([own, other]), jnp.stack([other, own]))


def gather_scaled(value, axis, scale):
    scaled = (value.astype(F32) * scale).astype(F16)
    return lax.all_gather(scaled, axis, axis=0, tiled=True)


def unscaled(value, scale):
    return (value.astype(F32) * (1.0 / scale)).astype(BF16)


def tn_dot(left, right):
    return lax.dot_general(left, right, (((0,), (0,)), ((), ())), preferred_element_type=F32)


def sum_kernel(parts_ref, out_ref):
    out_ref[0] = jnp.sum(parts_ref[:, :, 0].astype(F32), axis=0).astype(BF16)


def sum_by_tl(parts):
    return pl.pallas_call(
        sum_kernel,
        grid=(4,),
        in_specs=[pl.BlockSpec((4, 16, 1, 16, 256), lambda i: (0, 0, i, 0, 0))],
        out_specs=pl.BlockSpec((1, 16, 16, 256), lambda i: (i, 0, 0, 0)),
        out_shape=jax.ShapeDtypeStruct((4, 16, 16, 256), BF16),
        compiler_params=pltpu.CompilerParams(vmem_limit_bytes=16 * 2**20),
        cost_estimate=pl.CostEstimate(flops=2**20, bytes_accessed=5 * 2**19, transcendentals=0),
    )(parts.reshape(4, 16, 4, 16, 256))


def split_kernel(parts_ref, out_ref):
    added = jnp.sum(parts_ref[:, :, 0].astype(F32), axis=0).astype(BF16)
    out_ref[0, 0] = added[:, :, :128]
    out_ref[1, 0] = added[:, :, 128:]


def sum_by_zh_th(parts):
    return pl.pallas_call(
        split_kernel,
        grid=(2,),
        in_specs=[pl.BlockSpec((4, 8, 1, 16, 256), lambda i: (0, 0, i, 0, 0))],
        out_specs=pl.BlockSpec((2, 1, 8, 16, 128), lambda i: (0, i, 0, 0, 0)),
        out_shape=jax.ShapeDtypeStruct((2, 2, 8, 16, 128), BF16),
        compiler_params=pltpu.CompilerParams(vmem_limit_bytes=16 * 2**20),
        cost_estimate=pl.CostEstimate(flops=2**18, bytes_accessed=5 * 2**17, transcendentals=0),
    )(parts.reshape(4, 8, 2, 16, 256)).reshape(4, 128, 128)


def on_device(tokens_in, weight, grad_out):
    core, yl, zh, x, th, tl = (lax.axis_index(a) for a in ("core", "yl", "zh", "x", "th", "tl"))
    tok = th * 4 + tl
    piece = lax.axis_index(IN)

    with jax.named_scope("gather_quarter"):
        own = rows_of(tokens_in, x * 32, 32)
        own_grad = rows_of(grad_out, piece * 16, 16)
        keep = cols_of(own_grad, th * 2048, 2048).reshape(16, 4, 512)
        send = cols_of(own_grad, (1 - th) * 2048, 2048)
        send = jnp.concatenate([own, send[:, :1024], send[:, 1024:]], axis=0)
        got = swap(send, "th")
        got_grad = jnp.concatenate([got[32:48], got[48:]], axis=1).reshape(16, 4, 512)
        near_grad = both_th(keep, got_grad, th).transpose(2, 1, 0, 3).reshape(4, 16, 1024)
        near = both_th(own, got[:32], th).reshape(64, 1024)
        near = jnp.concatenate([jnp.broadcast_to(near[None], (4, 64, 1024)), near_grad], axis=1)
        near = exchange(near, "tl")
        quarter = near[:, :64].reshape(4, 2, 2, 16, 1024).transpose(2, 1, 0, 3, 4)
        grad_out_piece = near[:, 64:].reshape(4, 16, 2, 512).transpose(2, 0, 1, 3).reshape(128, 512)

    with jax.named_scope("gather_tokens"):
        quarter = quarter.reshape(256, 1024)
        tokens = unscaled(gather_scaled(quarter, "x", TOKEN_SCALE), TOKEN_SCALE)

    with jax.named_scope("act_columns"):
        act_start = x % 2 * 512
        act_own = lax.dynamic_slice(tokens, (core * 512, act_start), (512, 512))
        act_other = swap(lax.dynamic_slice(tokens, ((1 - core) * 512, act_start), (512, 512)), "core")

    with jax.named_scope("preact"):
        partial = jnp.dot(tokens, weight, preferred_element_type=F32).astype(F16)
        parts, act_other = lax.optimization_barrier(
            (exchange(partial.reshape(8, 128, 512), IN), act_other)
        )
        preact = total(parts)
        grad_piece = (grad_out_piece.astype(F32) * gelu_slope(preact)).astype(BF16)

    with jax.named_scope("gather_grad"):
        grad_rows = unscaled(gather_scaled(grad_piece, IN, GRAD_SCALE), GRAD_SCALE)

    with jax.named_scope("factor_columns"):
        away = tok ^ piece
        far = send_along(grad_rows, 4, (0,))
        cross = jnp.where(away == 0, grad_rows, far)

    with jax.named_scope("act_columns"):
        act_half = jnp.where(core == x // 2, act_own, act_other)
        from_y = swap(act_half, "yl")

    with jax.named_scope("grad_input"):
        by_x = weight.reshape(2, 4, 128, 512).transpose(1, 0, 2, 3).reshape(4, 256, 512)
        share = jnp.einsum("rc,kfc->krf", grad_rows, by_x, preferred_element_type=F32).astype(BF16)
        part, cross, from_y = lax.optimization_barrier((exchange(share, "x"), cross, from_y))
        mid = send_along(cross, 2, (0, 4))
        act_half = jnp.where(yl == zh, act_half, from_y)
        grad_weight = tn_dot(tokens, grad_rows).astype(BF16)
        part, mid, act_rest, grad_weight = lax.optimization_barrier(
            (exchange(sum_by_tl(part), "tl"), mid, swap(act_half, "core"), grad_weight)
        )
        part = exchange(sum_by_zh_th(part), ("zh", "th"))
        grad_input = total(part).astype(BF16)

    with jax.named_scope("grad_factor"):
        cross = jnp.where(away & 2 == 0, cross, mid)
        near = send_along(cross, 1, (0, 2, 4, 6))
        cross = jnp.where(away & 1 == 0, cross, near)
        grad_factor = tn_dot(grad_rows, cross) / 1024.0

    with jax.named_scope("act_factor"):
        act_rows = cols_of(tokens, tok * 128, 128)
        act_factor = tn_dot(rows_of(act_rows, core * 512, 512), act_half)
        act_factor += tn_dot(rows_of(act_rows, (1 - core) * 512, 512), act_rest)
        act_factor /= 1024.0
    return (grad_input, grad_weight, act_factor, grad_factor)


def solution(mesh):
    fine = Mesh(mesh.devices.reshape(2, 2, 2, 2, 4, 2, 4), IN + OUT + TOK)
    return jax.shard_map(
        on_device,
        mesh=fine,
        in_specs=(P(TOK, IN), P(IN, OUT + TOK), P(TOK, OUT)),
        out_specs=(P(TOK, IN + OUT), P(IN, OUT + TOK), P(IN + TOK, OUT), P(OUT + TOK, IN)),
        check_vma=False,
    )
```

```python
import math

import jax
import jax.numpy as jnp
from jax import lax
from jax.experimental import pallas as pl
from jax.experimental.pallas import tpu as pltpu
from jax.sharding import Mesh, PartitionSpec as P

BF16 = jnp.bfloat16
F16 = jnp.float16
F32 = jnp.float32
IN = ("yh", "yl", "core")
OUT = ("zh", "x")
TOK = ("th", "tl")
TOKEN_SCALE = 8192.0
GRAD_SCALE = 4096.0


def gelu_slope(values):
    scale = math.sqrt(2.0 / math.pi)
    cubic = values * values * values
    tanh_val = jnp.tanh(scale * (values + 0.044715 * cubic))
    return 0.5 * (1.0 + tanh_val) + 0.5 * values * (1.0 - tanh_val * tanh_val) * scale * (
        1.0 + 3.0 * 0.044715 * values * values
    )


def swap(value, axis):
    return lax.ppermute(value, axis, [(0, 1), (1, 0)])


def send_along(value, bits, before):
    pairs = []
    for i in range(8):
        holders = [0]
        for done in before:
            holders += [h ^ done[i % 2] for h in holders]
        pairs += [(i * 8 + (i ^ h), i * 8 + (i ^ h ^ bits[i % 2])) for h in holders]
    return lax.ppermute(value, IN + TOK, pairs)


def exchange(value, axis):
    return lax.all_to_all(value, axis, split_axis=0, concat_axis=0, tiled=True)


def total(parts):
    return jnp.sum(parts.astype(F32), axis=0)


def rows_of(value, start, size):
    return lax.dynamic_slice_in_dim(value, start, size, 0)


def cols_of(value, start, size):
    return lax.dynamic_slice_in_dim(value, start, size, 1)


def both_th(own, other, th):
    return jnp.where(th == 0, jnp.stack([own, other]), jnp.stack([other, own]))


def gather_scaled(value, axis, scale):
    scaled = (value.astype(F32) * scale).astype(F16)
    return lax.all_gather(scaled, axis, axis=0, tiled=True)


def unscaled(value, scale):
    return (value.astype(F32) * (1.0 / scale)).astype(BF16)


def tn_dot(left, right):
    return lax.dot_general(left, right, (((0,), (0,)), ((), ())), preferred_element_type=F32)


def sum_kernel(parts_ref, out_ref):
    out_ref[0] = jnp.sum(parts_ref[:, :, 0].astype(F32), axis=0).astype(BF16)


def sum_by_tl(parts):
    return pl.pallas_call(
        sum_kernel,
        grid=(4,),
        in_specs=[pl.BlockSpec((4, 16, 1, 16, 256), lambda i: (0, 0, i, 0, 0))],
        out_specs=pl.BlockSpec((1, 16, 16, 256), lambda i: (i, 0, 0, 0)),
        out_shape=jax.ShapeDtypeStruct((4, 16, 16, 256), BF16),
        compiler_params=pltpu.CompilerParams(vmem_limit_bytes=16 * 2**20),
        cost_estimate=pl.CostEstimate(flops=2**20, bytes_accessed=5 * 2**19, transcendentals=0),
    )(parts.reshape(4, 16, 4, 16, 256))


def split_kernel(parts_ref, out_ref):
    added = jnp.sum(parts_ref[:, :, 0].astype(F32), axis=0).astype(BF16)
    out_ref[0, 0] = added[:, :, :128]
    out_ref[1, 0] = added[:, :, 128:]


def sum_by_zh_th(parts):
    return pl.pallas_call(
        split_kernel,
        grid=(2,),
        in_specs=[pl.BlockSpec((4, 8, 1, 16, 256), lambda i: (0, 0, i, 0, 0))],
        out_specs=pl.BlockSpec((2, 1, 8, 16, 128), lambda i: (0, i, 0, 0, 0)),
        out_shape=jax.ShapeDtypeStruct((2, 2, 8, 16, 128), BF16),
        compiler_params=pltpu.CompilerParams(vmem_limit_bytes=16 * 2**20),
        cost_estimate=pl.CostEstimate(flops=2**18, bytes_accessed=5 * 2**17, transcendentals=0),
    )(parts.reshape(4, 8, 2, 16, 256)).reshape(4, 128, 128)


def on_device(tokens_in, weight, grad_out):
    core, yl, zh, x, th, tl = (lax.axis_index(a) for a in ("core", "yl", "zh", "x", "th", "tl"))
    tok = th * 4 + tl
    piece = lax.axis_index(IN)

    with jax.named_scope("gather_quarter"):
        own = rows_of(tokens_in, x * 32, 32)
        own_grad = rows_of(grad_out, piece * 16, 16)
        keep = cols_of(own_grad, th * 2048, 2048).reshape(16, 4, 512)
        send = cols_of(own_grad, (1 - th) * 2048, 2048)
        send = jnp.concatenate([own, send[:, :1024], send[:, 1024:]], axis=0)
        got = swap(send, "th")
        got_grad = jnp.concatenate([got[32:48], got[48:]], axis=1).reshape(16, 4, 512)
        near_grad = both_th(keep, got_grad, th).transpose(2, 1, 0, 3).reshape(4, 16, 1024)
        near = both_th(own, got[:32], th).reshape(64, 1024)
        near = jnp.concatenate([jnp.broadcast_to(near[None], (4, 64, 1024)), near_grad], axis=1)
        near = exchange(near, "tl")
        quarter = near[:, :64].reshape(4, 2, 2, 16, 1024).transpose(2, 1, 0, 3, 4)
        grad_out_piece = near[:, 64:].reshape(4, 16, 2, 512).transpose(2, 0, 1, 3).reshape(128, 512)

    with jax.named_scope("gather_tokens"):
        quarter = quarter.reshape(256, 1024)
        tokens = unscaled(gather_scaled(quarter, "x", TOKEN_SCALE), TOKEN_SCALE)

    with jax.named_scope("act_columns"):
        act_start = x % 2 * 512
        act_own = lax.dynamic_slice(tokens, (core * 512, act_start), (512, 512))
        act_other = swap(lax.dynamic_slice(tokens, ((1 - core) * 512, act_start), (512, 512)), "core")

    with jax.named_scope("preact"):
        partial = jnp.dot(tokens, weight, preferred_element_type=F32).astype(F16)
        parts, act_other = lax.optimization_barrier(
            (exchange(partial.reshape(8, 128, 512), IN), act_other)
        )
        preact = total(parts)
        grad_piece = (grad_out_piece.astype(F32) * gelu_slope(preact)).astype(BF16)

    with jax.named_scope("gather_grad"):
        grad_rows = unscaled(gather_scaled(grad_piece, IN, GRAD_SCALE), GRAD_SCALE)

    with jax.named_scope("factor_columns"):
        away = tok ^ piece
        far = send_along(grad_rows, (4, 4), ())
        cross = jnp.where(away == 0, grad_rows, far)

    with jax.named_scope("act_columns"):
        act_half = jnp.where(core == x // 2, act_own, act_other)
        from_y = swap(act_half, "yl")

    with jax.named_scope("grad_input"):
        by_x = weight.reshape(2, 4, 128, 512).transpose(1, 0, 2, 3).reshape(4, 256, 512)
        share = jnp.einsum("rc,kfc->krf", grad_rows, by_x, preferred_element_type=F32).astype(BF16)
        part, cross, from_y = lax.optimization_barrier((exchange(share, "x"), cross, from_y))
        mid = send_along(cross, (2, 1), ((4, 4),))
        act_half = jnp.where(yl == zh, act_half, from_y)
        grad_weight = tn_dot(tokens, grad_rows).astype(BF16)
        part, mid, act_rest, grad_weight = lax.optimization_barrier(
            (exchange(sum_by_tl(part), "tl"), mid, swap(act_half, "core"), grad_weight)
        )
        part = exchange(sum_by_zh_th(part), ("zh", "th"))
        grad_input = total(part).astype(BF16)

    with jax.named_scope("grad_factor"):
        cross = jnp.where(away & (2 - core) == 0, cross, mid)
        near = send_along(cross, (1, 2), ((4, 4), (2, 1)))
        cross = jnp.where(away & (1 + core) == 0, cross, near)
        grad_factor = tn_dot(grad_rows, cross) / 1024.0

    with jax.named_scope("act_factor"):
        act_rows = cols_of(tokens, tok * 128, 128)
        act_factor = tn_dot(rows_of(act_rows, core * 512, 512), act_half)
        act_factor += tn_dot(rows_of(act_rows, (1 - core) * 512, 512), act_rest)
        act_factor /= 1024.0
    return (grad_input, grad_weight, act_factor, grad_factor)


def solution(mesh):
    fine = Mesh(mesh.devices.reshape(2, 2, 2, 2, 4, 2, 4), IN + OUT + TOK)
    return jax.shard_map(
        on_device,
        mesh=fine,
        in_specs=(P(TOK, IN), P(IN, OUT + TOK), P(TOK, OUT)),
        out_specs=(P(TOK, IN + OUT), P(IN, OUT + TOK), P(IN + TOK, OUT), P(OUT + TOK, IN)),
        check_vma=False,
    )
```

```python
import math

import jax
import jax.numpy as jnp
from jax import lax
from jax.experimental import pallas as pl
from jax.experimental.pallas import tpu as pltpu
from jax.sharding import Mesh, PartitionSpec as P

BF16 = jnp.bfloat16
F16 = jnp.float16
F32 = jnp.float32
IN = ("yh", "yl", "core")
OUT = ("zh", "x")
TOK = ("th", "tl")
TOKEN_SCALE = 8192.0
GRAD_SCALE = 4096.0


def gelu_slope(values):
    scale = math.sqrt(2.0 / math.pi)
    cubic = values * values * values
    tanh_val = jnp.tanh(scale * (values + 0.044715 * cubic))
    return 0.5 * (1.0 + tanh_val) + 0.5 * values * (1.0 - tanh_val * tanh_val) * scale * (
        1.0 + 3.0 * 0.044715 * values * values
    )


def swap(value, axis):
    return lax.ppermute(value, axis, [(0, 1), (1, 0)])


def send_along(value, bit, holders):
    pairs = [(i * 8 + (i ^ h), i * 8 + (i ^ h ^ bit)) for i in range(8) for h in holders]
    return lax.ppermute(value, IN + TOK, pairs)


def exchange(value, axis):
    return lax.all_to_all(value, axis, split_axis=0, concat_axis=0, tiled=True)


def total(parts):
    return jnp.sum(parts.astype(F32), axis=0)


def rows_of(value, start, size):
    return lax.dynamic_slice_in_dim(value, start, size, 0)


def cols_of(value, start, size):
    return lax.dynamic_slice_in_dim(value, start, size, 1)


def both_th(own, other, th):
    return jnp.where(th == 0, jnp.stack([own, other]), jnp.stack([other, own]))


def gather_scaled(value, axis, scale):
    scaled = (value.astype(F32) * scale).astype(F16)
    return lax.all_gather(scaled, axis, axis=0, tiled=True)


def unscaled(value, scale):
    return (value.astype(F32) * (1.0 / scale)).astype(BF16)


def tn_dot(left, right):
    return lax.dot_general(left, right, (((0,), (0,)), ((), ())), preferred_element_type=F32)


def sum_kernel(parts_ref, out_ref):
    out_ref[0] = jnp.sum(parts_ref[:, :, 0].astype(F32), axis=0).astype(BF16)


def sum_by_tl(parts):
    return pl.pallas_call(
        sum_kernel,
        grid=(4,),
        in_specs=[pl.BlockSpec((4, 16, 1, 16, 256), lambda i: (0, 0, i, 0, 0))],
        out_specs=pl.BlockSpec((1, 16, 16, 256), lambda i: (i, 0, 0, 0)),
        out_shape=jax.ShapeDtypeStruct((4, 16, 16, 256), BF16),
        compiler_params=pltpu.CompilerParams(vmem_limit_bytes=16 * 2**20),
        cost_estimate=pl.CostEstimate(flops=2**20, bytes_accessed=5 * 2**19, transcendentals=0),
    )(parts.reshape(4, 16, 4, 16, 256))


def split_kernel(parts_ref, out_ref):
    added = jnp.sum(parts_ref[:, :, 0].astype(F32), axis=0).astype(BF16)
    out_ref[0, 0] = added[:, :, :128]
    out_ref[1, 0] = added[:, :, 128:]


def sum_by_zh_th(parts):
    return pl.pallas_call(
        split_kernel,
        grid=(2,),
        in_specs=[pl.BlockSpec((4, 8, 1, 16, 256), lambda i: (0, 0, i, 0, 0))],
        out_specs=pl.BlockSpec((2, 1, 8, 16, 128), lambda i: (0, i, 0, 0, 0)),
        out_shape=jax.ShapeDtypeStruct((2, 2, 8, 16, 128), BF16),
        compiler_params=pltpu.CompilerParams(vmem_limit_bytes=16 * 2**20),
        cost_estimate=pl.CostEstimate(flops=2**18, bytes_accessed=5 * 2**17, transcendentals=0),
    )(parts.reshape(4, 8, 2, 16, 256)).reshape(4, 128, 128)


def on_device(tokens_in, weight, grad_out):
    core, yl, zh, x, th, tl = (lax.axis_index(a) for a in ("core", "yl", "zh", "x", "th", "tl"))
    tok = th * 4 + tl
    piece = lax.axis_index(IN)

    with jax.named_scope("gather_quarter"):
        own = rows_of(tokens_in, x * 32, 32)
        own_grad = rows_of(grad_out, piece * 16, 16)
        keep = cols_of(own_grad, th * 2048, 2048).reshape(16, 4, 512)
        send = cols_of(own_grad, (1 - th) * 2048, 2048)
        send = jnp.concatenate([own, send[:, :1024], send[:, 1024:]], axis=0)
        got = swap(send, "th")
        got_grad = jnp.concatenate([got[32:48], got[48:]], axis=1).reshape(16, 4, 512)
        near_grad = both_th(keep, got_grad, th).transpose(2, 1, 0, 3).reshape(4, 16, 1024)
        near = both_th(own, got[:32], th).reshape(64, 1024)
        near = jnp.concatenate([jnp.broadcast_to(near[None], (4, 64, 1024)), near_grad], axis=1)
        near = exchange(near, "tl")
        quarter = near[:, :64].reshape(4, 2, 2, 16, 1024).transpose(2, 1, 0, 3, 4)
        grad_out_piece = near[:, 64:].reshape(4, 16, 2, 512).transpose(2, 0, 1, 3).reshape(128, 512)

    with jax.named_scope("gather_tokens"):
        quarter = quarter.reshape(256, 1024)
        tokens = unscaled(gather_scaled(quarter, "x", TOKEN_SCALE), TOKEN_SCALE)

    with jax.named_scope("act_columns"):
        act_start = x % 2 * 512
        act_own = lax.dynamic_slice(tokens, (core * 512, act_start), (512, 512))
        act_other = swap(lax.dynamic_slice(tokens, ((1 - core) * 512, act_start), (512, 512)), "core")

    with jax.named_scope("preact"):
        partial = jnp.dot(tokens, weight, preferred_element_type=F32).astype(F16)
        parts, act_other = lax.optimization_barrier(
            (exchange(partial.reshape(8, 128, 512), IN), act_other)
        )
        preact = total(parts)
        grad_piece = (grad_out_piece.astype(F32) * gelu_slope(preact)).astype(BF16)

    with jax.named_scope("gather_grad"):
        grad_rows = unscaled(gather_scaled(grad_piece, IN, GRAD_SCALE), GRAD_SCALE)

    with jax.named_scope("factor_columns"):
        away = tok ^ piece
        far = send_along(grad_rows, 4, (0,))
        cross = jnp.where(away == 0, grad_rows, far)
        mid = send_along(cross, 2, (0, 4))

    with jax.named_scope("act_columns"):
        act_half = jnp.where(core == x // 2, act_own, act_other)
        from_y = swap(act_half, "yl")

    with jax.named_scope("grad_input"):
        by_x = weight.reshape(2, 4, 128, 512).transpose(1, 0, 2, 3).reshape(4, 256, 512)
        share = jnp.einsum("rc,kfc->krf", grad_rows, by_x, preferred_element_type=F32).astype(BF16)
        part, from_y = lax.optimization_barrier((exchange(share, "x"), from_y))
        act_half = jnp.where(yl == zh, act_half, from_y)
        grad_weight = tn_dot(tokens, grad_rows).astype(BF16)
        part, cross, act_rest, grad_weight = lax.optimization_barrier(
            (exchange(sum_by_tl(part), "tl"), cross, swap(act_half, "core"), grad_weight)
        )
        part, mid = lax.optimization_barrier((exchange(sum_by_zh_th(part), ("zh", "th")), mid))
        grad_input = total(part).astype(BF16)

    with jax.named_scope("grad_factor"):
        cross = jnp.where(away & 2 == 0, cross, mid)
        near = send_along(cross, 1, (0, 2, 4, 6))
        cross = jnp.where(away & 1 == 0, cross, near)
        grad_factor = tn_dot(grad_rows, cross) / 1024.0

    with jax.named_scope("act_factor"):
        act_rows = cols_of(tokens, tok * 128, 128)
        act_factor = tn_dot(rows_of(act_rows, core * 512, 512), act_half)
        act_factor += tn_dot(rows_of(act_rows, (1 - core) * 512, 512), act_rest)
        act_factor /= 1024.0
    return (grad_input, grad_weight, act_factor, grad_factor)


def solution(mesh):
    fine = Mesh(mesh.devices.reshape(2, 2, 2, 2, 4, 2, 4), IN + OUT + TOK)
    return jax.shard_map(
        on_device,
        mesh=fine,
        in_specs=(P(TOK, IN), P(IN, OUT + TOK), P(TOK, OUT)),
        out_specs=(P(TOK, IN + OUT), P(IN, OUT + TOK), P(IN + TOK, OUT), P(OUT + TOK, IN)),
        check_vma=False,
    )
```
